256 devices in a mesh: prow: 16 (over y_hi, x, core), pcol: 16 (over z, y_lo).
Axes of the slice: x: 4, y: 4 (y_hi: 2, y_lo: 2; y = y_hi * 2 + y_lo), z: 8, core: 2. Of those that a mesh axis runs over, the one named last changes fastest.
Arguments:
- anc_inverse: bfloat16 [2, 1, 16, 256, 1, 16, 256], P(None, None, 'prow', None, None, 'pcol'), may hold values from -6 to 6
- factor_panel: bfloat16 [2, 1, 16, 256, 1, 16, 256], P(None, None, 'prow', None, None, 'pcol'), may hold values from -0.09375 to 0.09375
- diag_inverse: bfloat16 [2, 1, 16, 256, 1, 16, 256], P(None, None, 'pcol', None, None, 'prow'), may hold values from -6 to 6
- block_pattern: int32 [2, 16, 16], replicated, may hold values from 0 to 1, as said below
Outputs:
- sigma_off: bfloat16 [2, 1, 16, 256, 1, 16, 256], P(None, None, 'prow', None, None, 'pcol')
- sigma_diag: bfloat16 [2, 1, 16, 256, 1, 16, 256], P(None, None, 'pcol', None, None, 'prow')
The draws below stay inside these ranges and needn't reach their ends.
Inputs may be any that keep to these rules, and one draw needn't show every extreme that they name: `block_pattern`: symmetric in its last two dimensions, with ones on the diagonal.
All inputs are finite; a program needn't handle non-finite values.
Results may differ from the reference program's by a relative error of at most 0.0039.
Values may be sent and summed in bfloat16 or wider, within the bound.
No kernel may reach another device: no remote copies, remote signals or barrier semaphores. Data moves between devices by JAX's collectives and lax.ppermute only.
A program may use at most 64 MiB of HBM per device.

```python
import jax
import jax.numpy as jnp
from jax import lax

BLK = 256
W = 4096
ANC = 4096
SN = 2
AB = 16
WB = 16
N_PROW = 16
N_PCOL = 16


def draw_block_pattern(key, part):
    key = jax.random.fold_in(key, 7)
    blocks = ANC // BLK
    raw_draw = jax.random.randint(key, (SN, blocks, blocks), 0, 16)
    row_ids = lax.broadcasted_iota(jnp.int32, (SN, blocks, blocks), 1)
    col_ids = lax.broadcasted_iota(jnp.int32, (SN, blocks, blocks), 2)
    symmetric = jnp.where(row_ids <= col_ids, raw_draw, jnp.swapaxes(raw_draw, 1, 2))
    threshold = 4 + 12 * jnp.maximum(row_ids, col_ids) // blocks
    chosen = (symmetric < threshold) | (row_ids == col_ids)
    return jnp.where(chosen, 1, 0).astype(jnp.int32)


def shard_levels(key, dims, split, smallest, top_value):
    gain = 1.0
    for axis_at, parts in split:
        draws = jax.random.uniform(jax.random.fold_in(jax.random.fold_in(key, 6), axis_at), (parts,), jnp.float32, smallest / len(split), top_value / len(split))
        gain = gain * jnp.repeat(jnp.exp(draws), dims[axis_at] // parts).reshape((-1,) + (1,) * (len(dims) - 1 - axis_at))
    return gain


def centred(own_key, shape, width, bound, cuts=(), kind=jnp.bfloat16):
    values = width * jax.random.normal(own_key, shape, jnp.float32)
    if cuts:
        values = values * shard_levels(own_key, shape, cuts, -0.22, 0.18)
    return jnp.clip(values, -bound, bound).astype(kind)


def setup_inputs(seed: int = 0) -> dict:
    seeds = jax.random.split(jax.random.key(seed), 5)
    return {
        "anc_inverse": centred(seeds[0], (SN, AB // N_PROW, N_PROW, BLK, AB // N_PCOL, N_PCOL, BLK), 1.0, 6.0, ((2, 16), (5, 16))),
        "factor_panel": centred(seeds[1], (SN, AB // N_PROW, N_PROW, BLK, WB // N_PCOL, N_PCOL, BLK), ANC ** -0.5, 0.09375, ((2, 16), (5, 16))),
        "diag_inverse": centred(seeds[2], (SN, WB // N_PCOL, N_PCOL, BLK, WB // N_PROW, N_PROW, BLK), 1.0, 6.0, ((2, 16), (5, 16))),
        "block_pattern": draw_block_pattern(jax.random.fold_in(seeds[4], 71), 0),
    }


def reference(anc_inverse, factor_panel, diag_inverse, block_pattern):
    dense_mask = jnp.repeat(jnp.repeat(block_pattern, BLK, axis=1), BLK, axis=2)
    masked_inv = anc_inverse.reshape(SN, ANC, ANC)
    masked_inv = jnp.where(dense_mask != 0, masked_inv, jnp.zeros_like(masked_inv))
    factor_rows = factor_panel.reshape(SN, ANC, W)
    given_diag = diag_inverse.reshape(SN, W, W)
    off_list = []
    diag_list = []
    for supernode in range(SN):
        product = jnp.dot(masked_inv[supernode], factor_rows[supernode], preferred_element_type=jnp.float32)
        off_block = (-product).astype(jnp.bfloat16)
        inner_sum = jnp.dot(factor_rows[supernode].T, off_block, preferred_element_type=jnp.float32)
        diag_block = (given_diag[supernode].astype(jnp.float32) - inner_sum).astype(jnp.bfloat16)
        off_list.append(off_block)
        diag_list.append(diag_block)
    sigma_off = jnp.stack(off_list).reshape(factor_panel.shape)
    sigma_diag = jnp.stack(diag_list).reshape(diag_inverse.shape)
    return sigma_off, sigma_diag
```

```python
import jax
import jax.numpy as jnp
from jax import lax
from jax.sharding import PartitionSpec as P

NX = 4
NZ = 8


def row_perm(fn):
    pairs = []
    for i in range(16):
        yh, x, c = fn(i // 8, (i // 2) % NX, i % 2)
        pairs.append((i, yh * 8 + (x % NX) * 2 + c))
    return pairs


def col_perm(fn):
    pairs = []
    for i in range(16):
        z, yl = fn(i // 2, i % 2)
        pairs.append((i, (z % NZ) * 2 + yl))
    return pairs


def flip_perm(cross):
    pairs = []
    for p in range(16):
        for q in range(16):
            to_p = (q // 2) * 2 + (p % 2) ^ cross
            to_q = (p // 2) * 2 + q % 2
            pairs.append((p * 16 + q, to_p * 16 + to_q))
    return pairs


SWAP = col_perm(lambda z, yl: (z, 1 - yl))
UP = col_perm(lambda z, yl: (z + 1, yl))
DOWN = col_perm(lambda z, yl: (z - 1, yl))


def z_ring(piece):
    found = [(0, piece)]
    ahead = behind = piece
    for step in range(1, NZ // 2):
        ahead = lax.ppermute(ahead, "pcol", UP)
        behind = lax.ppermute(behind, "pcol", DOWN)
        found += [(-step, ahead), (step, behind)]
    half = piece.shape[0] // 2
    ahead = lax.ppermute(ahead[:half], "pcol", UP)
    behind = lax.ppermute(behind[half:], "pcol", DOWN)
    found.append((NZ // 2, jnp.concatenate([ahead, behind], axis=0)))
    return found


def on_device(anc_inverse, factor_panel, diag_inverse, block_pattern):
    p = lax.axis_index("prow")
    q = lax.axis_index("pcol")
    yh, x, c = p // 8, (p // 2) % NX, p % 2
    z, yl = q // 2, q % 2
    anc = anc_inverse.reshape(2, 256, 256)
    panel = factor_panel.reshape(2, 256, 256)
    diag = diag_inverse.reshape(2, 256, 256)
    keep = lax.dynamic_slice(block_pattern, (0, p, q), (2, 1, 1))
    masked = jnp.where(keep != 0, anc, jnp.zeros_like(anc))

    def mine(pair):
        return jnp.where(yl == 0, pair[0], pair[1])

    def other(pair):
        return jnp.where(yl == 0, pair[1], pair[0])

    def swap(block):
        return lax.ppermute(block, "pcol", SWAP)

    own_m, got_m = mine(masked), swap(other(masked))
    own_u, got_u = mine(panel), swap(other(panel))
    same = yl == c
    m_piece = jnp.concatenate(
        [jnp.where(same, own_m, got_m), jnp.where(same, got_m, own_m)], axis=1
    )
    u_piece = jnp.concatenate(
        [jnp.where(yl == 0, own_u, got_u), jnp.where(yl == 0, got_u, own_u)], axis=1
    )
    u_far = lax.ppermute(u_piece, "prow", row_perm(lambda h, x, c: (1 - h, x, c)))
    both = jnp.stack([u_piece, u_far])
    groups = [both]
    for step in range(1, NX):
        groups.append(
            lax.ppermute(both, "prow", row_perm(lambda h, x, c: (h, x + step, c)))
        )
    cross = row_perm(lambda h, x, c: (h, x, 1 - c))
    u_all = jnp.stack([jnp.stack([g, lax.ppermute(g, "prow", cross)]) for g in groups])

    def u_rows(offset):
        owner = (z + offset + NZ) % NZ
        back = (x - owner % NX + NX) % NX
        away = jnp.where(owner // NX == yh, 0, 1)
        return lax.dynamic_slice(
            u_all, (back, 0, away, 0, 0), (1, 2, 1, 256, 512)
        ).reshape(512, 512)

    product = jnp.zeros((256, 512), jnp.float32)
    for offset, piece in z_ring(m_piece):
        product += jnp.dot(piece, u_rows(offset), preferred_element_type=jnp.float32)
    off = (-product).astype(jnp.bfloat16)
    left, right = off[:, :256], off[:, 256:]
    off_mine = jnp.where(yl == 0, left, right)
    off_got = swap(jnp.where(yl == 0, right, left))
    same_core = lax.ppermute(
        jnp.where(c == 0, left, right), ("prow", "pcol"), flip_perm(0)
    )
    cross_core = lax.ppermute(
        jnp.where(c == 0, right, left), ("prow", "pcol"), flip_perm(1)
    )
    o_piece = jnp.concatenate([same_core, cross_core], axis=0)
    inner = jnp.zeros((512, 256), jnp.float32)
    for offset, piece in z_ring(o_piece):
        inner += lax.dot_general(
            u_rows(offset),
            piece,
            (((0,), (0,)), ((), ())),
            preferred_element_type=jnp.float32,
        )
    d_mine, d_got = mine(diag), swap(other(diag))
    top, bottom = inner[:256], inner[256:]
    diag_mine = (
        d_mine.astype(jnp.float32) - jnp.where(yl == 0, top, bottom)
    ).astype(jnp.bfloat16)
    diag_got = swap(
        (d_got.astype(jnp.float32) - jnp.where(yl == 0, bottom, top)).astype(
            jnp.bfloat16
        )
    )

    def place(own, got):
        return jnp.stack(
            [jnp.where(yl == 0, own, got), jnp.where(yl == 0, got, own)]
        ).reshape(anc_inverse.shape)

    return place(off_mine, off_got), place(diag_mine, diag_got)


def solution(mesh):
    return jax.shard_map(
        on_device,
        mesh=mesh,
        in_specs=(
            P(None, None, "prow", None, None, "pcol", None),
            P(None, None, "prow", None, None, "pcol", None),
            P(None, None, "pcol", None, None, "prow", None),
            P(),
        ),
        out_specs=(
            P(None, None, "prow", None, None, "pcol", None),
            P(None, None, "pcol", None, None, "prow", None),
        ),
        check_vma=False,
    )
```

```python
import jax
import jax.numpy as jnp
from jax import lax
from jax.sharding import PartitionSpec as P

NX = 4
NZ = 8


def row_perm(fn):
    pairs = []
    for i in range(16):
        yh, x, c = fn(i // 8, (i // 2) % NX, i % 2)
        pairs.append((i, yh * 8 + (x % NX) * 2 + c))
    return pairs


def col_perm(fn):
    pairs = []
    for i in range(16):
        z, yl = fn(i // 2, i % 2)
        pairs.append((i, (z % NZ) * 2 + yl))
    return pairs


def both_perm(fn):
    pairs = []
    for p in range(16):
        for q in range(16):
            chip, c, z, yl = fn(p // 2, p % 2, q // 2, q % 2)
            pairs.append((p * 16 + q, (chip * 2 + c) * 16 + (z % NZ) * 2 + yl))
    return pairs


def move(block, pairs):
    return lax.ppermute(block, ("prow", "pcol"), pairs)


SWAP = col_perm(lambda z, yl: (z, 1 - yl))
UP = col_perm(lambda z, yl: (z + 1, yl))
DOWN = col_perm(lambda z, yl: (z - 1, yl))
CROSS = row_perm(lambda h, x, c: (h, x, 1 - c))
FLIP_H = row_perm(lambda h, x, c: (1 - h, x, c))
SPLIT = both_perm(lambda chip, c, z, yl: (chip, c, z + 1 - 2 * c, yl))


def z_ring(piece, core, beside=()):
    found = [(0, piece)]
    swapped = []
    ahead = behind = piece
    for step in range(1, NZ // 2):
        hold = None
        if 2 <= step < 2 + len(beside):
            ahead, behind, hold = lax.optimization_barrier(
                (ahead, behind, beside[step - 2])
            )
            swapped.append(lax.ppermute(hold, "pcol", SWAP))
        ahead = lax.ppermute(ahead, "pcol", UP)
        behind = lax.ppermute(behind, "pcol", DOWN)
        if hold is not None:
            ahead, behind, swapped[-1] = lax.optimization_barrier(
                (ahead, behind, swapped[-1])
            )
        found += [(-step, ahead), (step, behind)]
    found.append((NZ // 2, move(jnp.where(core == 0, ahead, behind), SPLIT)))
    return found, swapped


def on_device(anc_inverse, factor_panel, diag_inverse, block_pattern):
    p = lax.axis_index("prow")
    q = lax.axis_index("pcol")
    yh, x, c = p // 8, (p // 2) % NX, p % 2
    z, yl = q // 2, q % 2
    anc = anc_inverse.reshape(2, 256, 256)
    panel = factor_panel.reshape(2, 256, 256)
    diag = diag_inverse.reshape(2, 256, 256)

    def mine(pair):
        return jnp.where(yl == 0, pair[0], pair[1])

    def other(pair):
        return jnp.where(yl == 0, pair[1], pair[0])

    def swap(block):
        return lax.ppermute(block, "pcol", SWAP)

    near = move(
        jnp.where(c == 0, anc[0], anc[1]),
        both_perm(lambda chip, c, z, yl: (chip, yl, z, c)),
    )
    far = move(
        jnp.where(c == 0, anc[1], anc[0]),
        both_perm(lambda chip, c, z, yl: (chip, yl, z, 1 - c)),
    )
    keep = lax.dynamic_slice(block_pattern, (yl, p - c, 2 * z + c), (1, 2, 1))
    keep = jnp.where(yl == 0, keep, keep[:, ::-1]).reshape(2, 1, 1) != 0
    m_piece = jnp.stack([near, far])
    m_piece = jnp.where(keep, m_piece, jnp.zeros_like(m_piece)).reshape(512, 256)

    own_u, got_u = mine(panel), swap(other(panel))
    u_piece = jnp.concatenate(
        [jnp.where(yl == 0, own_u, got_u), jnp.where(yl == 0, got_u, own_u)], axis=1
    )

    def along_x(block, step):
        return lax.ppermute(block, "prow", row_perm(lambda h, x, c: (h, x + step, c)))

    u_far = lax.ppermute(u_piece, "prow", FLIP_H)
    u_two = along_x(u_piece, 2)
    both = jnp.stack([u_piece, u_far])
    u_one = along_x(both, 1)
    u_three = along_x(both, 3)
    u_two_far = lax.ppermute(u_two, "prow", FLIP_H)
    u_all = jnp.zeros((NX, 2, 256, 512), jnp.bfloat16)
    for back, away, block in (
        (0, 0, both),
        (2, 0, u_two[None]),
        (2, 1, u_two_far[None]),
        (1, 0, u_one),
        (3, 0, u_three),
    ):
        u_all = lax.dynamic_update_slice(u_all, block[None], (back, away, 0, 0))

    def find(offset):
        owner = (z + offset + NZ) % NZ
        back = (x - owner % NX + NX) % NX
        return back, jnp.where(owner // NX == yh, 0, 1)

    def u_rows(offset):
        at = (*find(offset), 0, 0)
        return lax.dynamic_slice(u_all, at, (1, 1, 256, 512)).reshape(256, 512)

    product = jnp.zeros((512, 512), jnp.float32)
    for offset, piece in z_ring(m_piece, c)[0]:
        product += jnp.dot(piece, u_rows(offset), preferred_element_type=jnp.float32)
    first, second = product[:256], product[256:]
    theirs = lax.ppermute(jnp.where(yl == c, second, first), "prow", CROSS)
    off = (-(jnp.where(yl == c, first, second) + theirs)).astype(jnp.bfloat16)
    left, right = off[:, :256], off[:, 256:]
    off_mine = jnp.where(yl == 0, left, right)

    u_both = jnp.stack([u_all, lax.ppermute(u_all, "prow", CROSS)], axis=2)

    def u_pair(offset):
        at = (*find(offset), 0, 0, 0)
        return lax.dynamic_slice(u_both, at, (1, 1, 2, 256, 512)).reshape(512, 512)

    straight = move(
        jnp.where(c == 0, left, right),
        both_perm(lambda chip, c, z, yl: (z, c, chip, yl)),
    )
    around = lax.ppermute(jnp.where(c == 0, right, left), "prow", FLIP_H)
    around = move(around, both_perm(lambda chip, c, z, yl: (z, 1 - c, chip ^ 4, yl)))
    o_piece = jnp.concatenate([straight, around], axis=0)
    ring, (off_got, d_got) = z_ring(
        o_piece, c, (jnp.where(yl == 0, right, left), other(diag))
    )
    d_mine = mine(diag)
    total = jnp.zeros((512, 256), jnp.float32)
    for offset, piece in ring:
        total += lax.dot_general(
            u_pair(offset),
            piece,
            (((0,), (0,)), ((), ())),
            preferred_element_type=jnp.float32,
        )
    top, bottom = total[:256], total[256:]
    diag_mine = (
        d_mine.astype(jnp.float32) - jnp.where(yl == 0, top, bottom)
    ).astype(jnp.bfloat16)
    diag_got = swap(
        (d_got.astype(jnp.float32) - jnp.where(yl == 0, bottom, top)).astype(
            jnp.bfloat16
        )
    )

    def place(own, got):
        return jnp.stack(
            [jnp.where(yl == 0, own, got), jnp.where(yl == 0, got, own)]
        ).reshape(anc_inverse.shape)

    return place(off_mine, off_got), place(diag_mine, diag_got)


def solution(mesh):
    return jax.shard_map(
        on_device,
        mesh=mesh,
        in_specs=(
            P(None, None, "prow", None, None, "pcol", None),
            P(None, None, "prow", None, None, "pcol", None),
            P(None, None, "pcol", None, None, "prow", None),
            P(),
        ),
        out_specs=(
            P(None, None, "prow", None, None, "pcol", None),
            P(None, None, "pcol", None, None, "prow", None),
        ),
        check_vma=False,
    )
```

```python
import jax
import jax.numpy as jnp
from jax import lax
from jax.sharding import PartitionSpec as P

NX = 4
NZ = 8


def row_perm(fn):
    pairs = []
    for i in range(16):
        yh, x, c = fn(i // 8, (i // 2) % NX, i % 2)
        pairs.append((i, yh * 8 + (x % NX) * 2 + c))
    return pairs


def col_perm(fn):
    pairs = []
    for i in range(16):
        z, yl = fn(i // 2, i % 2)
        pairs.append((i, (z % NZ) * 2 + yl))
    return pairs


def both_perm(fn):
    pairs = []
    for p in range(16):
        for q in range(16):
            chip, c, z, yl = fn(p // 2, p % 2, q // 2, q % 2)
            pairs.append((p * 16 + q, (chip * 2 + c) * 16 + (z % NZ) * 2 + yl))
    return pairs


def move(block, pairs):
    return lax.ppermute(block, ("prow", "pcol"), pairs)


SWAP = col_perm(lambda z, yl: (z, 1 - yl))
UP = col_perm(lambda z, yl: (z + 1, yl))
DOWN = col_perm(lambda z, yl: (z - 1, yl))
OPPOSITE = col_perm(lambda z, yl: (z + NZ // 2, yl))
CROSS = row_perm(lambda h, x, c: (h, x, 1 - c))
FLIP_H = row_perm(lambda h, x, c: (1 - h, x, c))
SPLIT = both_perm(lambda chip, c, z, yl: (chip, c, z + 1 - 2 * c, yl))


def up(block):
    return lax.ppermute(block, "pcol", UP)


def down(block):
    return lax.ppermute(block, "pcol", DOWN)


def tie(*values):
    return lax.optimization_barrier(values)


def z_ring(piece, core, add, total, beside=()):
    swapped = []
    ahead = behind = piece
    found = [(0, piece)]
    for step in range(1, NZ // 2):
        near = found
        if 2 <= step < 2 + len(beside):
            ahead, behind, hold = tie(ahead, behind, beside[step - 2])
            swapped.append(lax.ppermute(hold, "pcol", SWAP))
        ahead, behind = up(ahead), down(behind)
        found = [(-step, ahead), (step, behind)]
        for offset, block in near:
            total = add(total, offset, block)
        if beside:
            ahead, behind, total = tie(ahead, behind, total)
        if 2 <= step < 2 + len(beside):
            ahead, behind, swapped[-1] = tie(ahead, behind, swapped[-1])
    last = move(jnp.where(core == 0, ahead, behind), SPLIT)
    for offset, block in found:
        total = add(total, offset, block)
    return add(total, NZ // 2, last), swapped


def on_device(anc_inverse, factor_panel, diag_inverse, block_pattern):
    p = lax.axis_index("prow")
    q = lax.axis_index("pcol")
    yh, x, c = p // 8, (p // 2) % NX, p % 2
    z, yl = q // 2, q % 2
    anc = anc_inverse.reshape(2, 256, 256)
    panel = factor_panel.reshape(2, 256, 256)
    diag = diag_inverse.reshape(2, 256, 256)

    def mine(pair):
        return jnp.where(yl == 0, pair[0], pair[1])

    def other(pair):
        return jnp.where(yl == 0, pair[1], pair[0])

    def swap(block):
        return lax.ppermute(block, "pcol", SWAP)

    near = move(
        jnp.where(c == 0, anc[0], anc[1]),
        both_perm(lambda chip, c, z, yl: (chip, yl, z, c)),
    )
    far = move(
        jnp.where(c == 0, anc[1], anc[0]),
        both_perm(lambda chip, c, z, yl: (chip, yl, z, 1 - c)),
    )
    oth_u, near = tie(other(panel), near)
    own_u, got_u = mine(panel), swap(oth_u)
    same = yl == c
    keep = lax.dynamic_slice(block_pattern, (yl, p - c, 2 * z + c), (1, 2, 1))
    keep = jnp.where(c == 0, keep, keep[:, ::-1]).reshape(2, 1, 1) != 0
    m_piece = jnp.where(same, jnp.stack([near, far]), jnp.stack([far, near]))
    m_piece = jnp.where(keep, m_piece, jnp.zeros_like(m_piece)).reshape(512, 256)

    u_piece = jnp.concatenate(
        [jnp.where(same, own_u, got_u), jnp.where(same, got_u, own_u)], axis=1
    )

    def along_x(block, step):
        return lax.ppermute(block, "prow", row_perm(lambda h, x, c: (h, x + step, c)))

    u_far = lax.ppermute(u_piece, "prow", FLIP_H)
    u_two = along_x(u_piece, 2)
    both = jnp.stack([u_piece, u_far])
    u_one = along_x(both, 1)
    u_three = along_x(both, 3)
    u_two_far = lax.ppermute(u_two, "prow", FLIP_H)
    u_all = jnp.zeros((NX, 2, 256, 512), jnp.bfloat16)
    for back, away, block in (
        (0, 0, both),
        (2, 0, u_two[None]),
        (2, 1, u_two_far[None]),
        (1, 0, u_one),
        (3, 0, u_three),
    ):
        u_all = lax.dynamic_update_slice(u_all, block[None], (back, away, 0, 0))

    def find(owner):
        owner = (owner + NZ) % NZ
        back = (x - owner % NX + NX) % NX
        return back, jnp.where(owner // NX == yh, 0, 1)

    def u_rows(panel, owner):
        at = (*find(owner), 0, 0)
        return lax.dynamic_slice(panel, at, (1, 1, 256, 512)).reshape(256, 512)

    def add_product(total, offset, block):
        rows = u_rows(u_all, z + offset)
        return tuple(
            part + jnp.dot(block, cols, preferred_element_type=jnp.float32)
            for part, cols in zip(total, (rows[:, :256], rows[:, 256:]))
        )

    zero = jnp.zeros((512, 256), jnp.float32)
    (kept, sent), _ = z_ring(m_piece, c, add_product, (zero, zero))
    theirs = lax.ppermute(sent, "prow", CROSS)
    off = kept + jnp.concatenate([theirs[256:], theirs[:256]], axis=0)
    off = (-off).astype(jnp.bfloat16)

    o_piece = move(off, both_perm(lambda chip, c, z, yl: (z, c, chip - z, yl)))
    u_cross = lax.ppermute(u_all, "prow", CROSS)
    o_piece, u_cross = tie(o_piece, u_cross)
    first, second = off[:256], lax.ppermute(off[256:], "prow", CROSS)
    off_mine = jnp.where(same, first, second)

    def add_inner(total, offset, block):
        return tuple(
            part
            + lax.dot_general(
                u_rows(panel, p // 2 + z + offset),
                rows,
                (((0,), (0,)), ((), ())),
                preferred_element_type=jnp.float32,
            )
            for part, panel, rows in zip(
                total, (u_all, u_cross), (block[:256], block[256:])
            )
        )

    total, (off_got, d_got) = z_ring(
        o_piece, c, add_inner, (zero, zero), (jnp.where(same, second, first), other(diag))
    )
    first = total[0][:256] + total[1][256:]
    second = total[0][256:] + total[1][:256]
    d_mine = mine(diag)
    diag_mine = (
        d_mine.astype(jnp.float32) - jnp.where(same, first, second)
    ).astype(jnp.bfloat16)
    diag_got = swap(
        (d_got.astype(jnp.float32) - jnp.where(same, second, first)).astype(
            jnp.bfloat16
        )
    )

    def place(own, got):
        return jnp.stack(
            [jnp.where(yl == 0, own, got), jnp.where(yl == 0, got, own)]
        ).reshape(anc_inverse.shape)

    return place(off_mine, off_got), place(diag_mine, diag_got)


def solution(mesh):
    return jax.shard_map(
        on_device,
        mesh=mesh,
        in_specs=(
            P(None, None, "prow", None, None, "pcol", None),
            P(None, None, "prow", None, None, "pcol", None),
            P(None, None, "pcol", None, None, "prow", None),
            P(),
        ),
        out_specs=(
            P(None, None, "prow", None, None, "pcol", None),
            P(None, None, "pcol", None, None, "prow", None),
        ),
        check_vma=False,
    )
```

```python
import jax
import jax.numpy as jnp
from jax import lax
from jax.sharding import PartitionSpec as P

NX = 4
NZ = 8


def row_perm(fn):
    pairs = []
    for i in range(16):
        yh, x, c = fn(i // 8, (i // 2) % NX, i % 2)
        pairs.append((i, yh * 8 + (x % NX) * 2 + c))
    return pairs


def col_perm(fn):
    pairs = []
    for i in range(16):
        z, yl = fn(i // 2, i % 2)
        pairs.append((i, (z % NZ) * 2 + yl))
    return pairs


def both_perm(fn):
    pairs = []
    for p in range(16):
        for q in range(16):
            chip, c, z, yl = fn(p // 2, p % 2, q // 2, q % 2)
            pairs.append((p * 16 + q, (chip * 2 + c) * 16 + (z % NZ) * 2 + yl))
    return pairs


LAND = (
    (0, 5, 7, 2, 1, 4, 6, 7),
    (6, 3, 1, 0, 6, 7, 1, 0),
    (7, 2, 0, 1, 3, 2, 0, 1),
    (5, 4, 2, 7, 4, 5, 7, 2),
    (2, 7, 4, 5, 7, 6, 5, 4),
    (1, 0, 6, 3, 5, 0, 2, 3),
    (4, 1, 3, 6, 0, 1, 3, 6),
    (3, 6, 5, 4, 2, 3, 4, 5),
)
LANDED = [
    sum(p << (3 * LAND[p][col]) for p in range(NZ)) for col in range(NZ)
]


def move(block, pairs):
    return lax.ppermute(block, ("prow", "pcol"), pairs)


SWAP = col_perm(lambda z, yl: (z, 1 - yl))
UP = col_perm(lambda z, yl: (z + 1, yl))
DOWN = col_perm(lambda z, yl: (z - 1, yl))
OPPOSITE = col_perm(lambda z, yl: (z + NZ // 2, yl))
CROSS = row_perm(lambda h, x, c: (h, x, 1 - c))
FLIP_H = row_perm(lambda h, x, c: (1 - h, x, c))
SPLIT = both_perm(lambda chip, c, z, yl: (chip, c, z + 1 - 2 * c, yl))


def up(block):
    return lax.ppermute(block, "pcol", UP)


def down(block):
    return lax.ppermute(block, "pcol", DOWN)


def tie(*values):
    return lax.optimization_barrier(values)


def z_ring(piece, core, add, total, beside=()):
    swapped = []
    ahead = behind = piece
    found = [(0, piece)]
    for step in range(1, NZ // 2):
        near = found
        if 2 <= step < 2 + len(beside):
            ahead, behind, hold = tie(ahead, behind, beside[step - 2])
            swapped.append(lax.ppermute(hold, "pcol", SWAP))
        ahead, behind = up(ahead), down(behind)
        found = [(-step, ahead), (step, behind)]
        for offset, block in near:
            total = add(total, offset, block)
        if beside:
            ahead, behind, total = tie(ahead, behind, total)
        if 2 <= step < 2 + len(beside):
            ahead, behind, swapped[-1] = tie(ahead, behind, swapped[-1])
    last = move(jnp.where(core == 0, ahead, behind), SPLIT)
    for offset, block in found:
        total = add(total, offset, block)
    return add(total, NZ // 2, last), swapped


def z_two(piece, opposite, add, total, beside):
    one = up(piece), down(piece)
    three = up(opposite), down(opposite)
    total = add(total, 0, piece)
    *one, total = tie(*one, total)
    two = up(one[0]), down(one[1])
    swapped = []
    for block, after in zip(beside, one):
        block, _ = tie(block, after)
        swapped.append(lax.ppermute(block, "pcol", SWAP))
    total = add(total, NZ // 2, opposite)
    for offset, blocks in ((1, one), (-3, three), (2, two)):
        total = add(total, -offset, blocks[0])
        total = add(total, offset, blocks[1])
    return total, swapped


def on_device(anc_inverse, factor_panel, diag_inverse, block_pattern):
    p = lax.axis_index("prow")
    q = lax.axis_index("pcol")
    yh, x, c = p // 8, (p // 2) % NX, p % 2
    z, yl = q // 2, q % 2
    anc = anc_inverse.reshape(2, 256, 256)
    panel = factor_panel.reshape(2, 256, 256)
    diag = diag_inverse.reshape(2, 256, 256)

    def mine(pair):
        return jnp.where(yl == 0, pair[0], pair[1])

    def other(pair):
        return jnp.where(yl == 0, pair[1], pair[0])

    def swap(block):
        return lax.ppermute(block, "pcol", SWAP)

    near = move(
        jnp.where(c == 0, anc[0], anc[1]),
        both_perm(lambda chip, c, z, yl: (chip, yl, z, c)),
    )
    far = move(
        jnp.where(c == 0, anc[1], anc[0]),
        both_perm(lambda chip, c, z, yl: (chip, yl, z, 1 - c)),
    )
    oth_u, near = tie(other(panel), near)
    own_u, got_u = mine(panel), swap(oth_u)
    same = yl == c
    keep = lax.dynamic_slice(block_pattern, (yl, p - c, 2 * z + c), (1, 2, 1))
    keep = jnp.where(c == 0, keep, keep[:, ::-1]).reshape(2, 1, 1) != 0
    m_piece = jnp.where(same, jnp.stack([near, far]), jnp.stack([far, near]))
    m_piece = jnp.where(keep, m_piece, jnp.zeros_like(m_piece)).reshape(512, 256)

    u_piece = jnp.concatenate(
        [jnp.where(same, own_u, got_u), jnp.where(same, got_u, own_u)], axis=1
    )

    def along_x(block, step):
        return lax.ppermute(block, "prow", row_perm(lambda h, x, c: (h, x + step, c)))

    u_far = lax.ppermute(u_piece, "prow", FLIP_H)
    u_two = along_x(u_piece, 2)
    both = jnp.stack([u_piece, u_far])
    u_one = along_x(both, 1)
    u_three = along_x(both, 3)
    u_two_far = lax.ppermute(u_two, "prow", FLIP_H)
    u_all = jnp.zeros((NX, 2, 256, 512), jnp.bfloat16)
    for back, away, block in (
        (0, 0, both),
        (2, 0, u_two[None]),
        (2, 1, u_two_far[None]),
        (1, 0, u_one),
        (3, 0, u_three),
    ):
        u_all = lax.dynamic_update_slice(u_all, block[None], (back, away, 0, 0))

    def find(owner):
        owner = (owner + NZ) % NZ
        back = (x - owner % NX + NX) % NX
        return back, jnp.where(owner // NX == yh, 0, 1)

    def u_rows(panel, owner):
        at = (*find(owner), 0, 0)
        return lax.dynamic_slice(panel, at, (1, 1, 256, 512)).reshape(256, 512)

    def add_product(total, offset, block):
        rows = u_rows(u_all, z + offset)
        return tuple(
            part + jnp.dot(block, cols, preferred_element_type=jnp.float32)
            for part, cols in zip(total, (rows[:, :256], rows[:, 256:]))
        )

    zero = jnp.zeros((512, 256), jnp.float32)
    (kept, sent), _ = z_ring(m_piece, c, add_product, (zero, zero))
    theirs = lax.ppermute(sent, "prow", CROSS)
    off = kept + jnp.concatenate([theirs[256:], theirs[:256]], axis=0)
    off = (-off).astype(jnp.bfloat16)

    o_piece = move(off, both_perm(lambda chip, c, z, yl: (z, c, LAND[chip][z], yl)))
    o_other = move(off, both_perm(lambda chip, c, z, yl: (z, c, LAND[chip][z] + 4, yl)))
    u_cross = lax.ppermute(u_all, "prow", CROSS)
    o_piece, o_other, u_cross = tie(o_piece, o_other, u_cross)
    (u_cross,) = tie(jnp.where(p >= 0, u_cross, jnp.zeros_like(u_cross)))
    first, second = off[:256], lax.ppermute(off[256:], "prow", CROSS)
    off_mine = jnp.where(same, first, second)

    landed = sum(
        jnp.where(p // 2 == col, parts, 0) for col, parts in enumerate(LANDED)
    )

    def add_inner(total, offset, block):
        owner = (landed >> (3 * ((z + offset + NZ) % NZ))) & 7
        return tuple(
            part
            + lax.dot_general(
                u_rows(panel, owner),
                rows,
                (((0,), (0,)), ((), ())),
                preferred_element_type=jnp.float32,
            )
            for part, panel, rows in zip(
                total, (u_all, u_cross), (block[:256], block[256:])
            )
        )

    total, (off_got, d_got) = z_two(
        o_piece, o_other, add_inner, (zero, zero), (jnp.where(same, second, first), other(diag))
    )
    first = total[0][:256] + total[1][256:]
    second = total[0][256:] + total[1][:256]
    d_mine = mine(diag)
    diag_mine = (
        d_mine.astype(jnp.float32) - jnp.where(same, first, second)
    ).astype(jnp.bfloat16)
    diag_got = swap(
        (d_got.astype(jnp.float32) - jnp.where(same, second, first)).astype(
            jnp.bfloat16
        )
    )

    def place(own, got):
        return jnp.stack(
            [jnp.where(yl == 0, own, got), jnp.where(yl == 0, got, own)]
        ).reshape(anc_inverse.shape)

    return place(off_mine, off_got), place(diag_mine, diag_got)


def solution(mesh):
    return jax.shard_map(
        on_device,
        mesh=mesh,
        in_specs=(
            P(None, None, "prow", None, None, "pcol", None),
            P(None, None, "prow", None, None, "pcol", None),
            P(None, None, "pcol", None, None, "prow", None),
            P(),
        ),
        out_specs=(
            P(None, None, "prow", None, None, "pcol", None),
            P(None, None, "pcol", None, None, "prow", None),
        ),
        check_vma=False,
    )
```

```python
import jax
import jax.numpy as jnp
from jax import lax
from jax.sharding import PartitionSpec as P

NX = 4
NZ = 8


def row_perm(fn):
    pairs = []
    for i in range(16):
        yh, x, c = fn(i // 8, (i // 2) % NX, i % 2)
        pairs.append((i, yh * 8 + (x % NX) * 2 + c))
    return pairs


def col_perm(fn):
    pairs = []
    for i in range(16):
        z, yl = fn(i // 2, i % 2)
        pairs.append((i, (z % NZ) * 2 + yl))
    return pairs


def both_perm(fn):
    pairs = []
    for p in range(16):
        for q in range(16):
            chip, c, z, yl = fn(p // 2, p % 2, q // 2, q % 2)
            pairs.append((p * 16 + q, (chip * 2 + c) * 16 + (z % NZ) * 2 + yl))
    return pairs


LAND = (
    (1, 4, 7, 6, 1, 0, 3, 2),
    (7, 6, 1, 4, 2, 3, 0, 1),
    (6, 5, 0, 7, 3, 1, 2, 0),
    (4, 3, 6, 1, 4, 6, 1, 7),
    (3, 1, 2, 0, 7, 5, 6, 4),
    (0, 2, 3, 5, 6, 7, 5, 3),
    (5, 7, 4, 2, 5, 4, 7, 6),
    (2, 0, 5, 3, 0, 2, 4, 5),
)
LANDED = [
    sum(p << (3 * LAND[p][col]) for p in range(NZ)) for col in range(NZ)
]


def move(block, pairs):
    return lax.ppermute(block, ("prow", "pcol"), pairs)


SWAP = col_perm(lambda z, yl: (z, 1 - yl))
UP = col_perm(lambda z, yl: (z + 1, yl))
DOWN = col_perm(lambda z, yl: (z - 1, yl))
OPPOSITE = col_perm(lambda z, yl: (z + NZ // 2, yl))
CROSS = row_perm(lambda h, x, c: (h, x, 1 - c))
FLIP_H = row_perm(lambda h, x, c: (1 - h, x, c))
SPLIT = both_perm(lambda chip, c, z, yl: (chip, c, z + 1 - 2 * c, yl))


def up(block):
    return lax.ppermute(block, "pcol", UP)


def down(block):
    return lax.ppermute(block, "pcol", DOWN)


def tie(*values):
    return lax.optimization_barrier(values)


def z_ring(piece, core, add, total, beside=()):
    swapped = []
    ahead = behind = piece
    found = [(0, piece)]
    for step in range(1, NZ // 2):
        near = found
        if 2 <= step < 2 + len(beside):
            ahead, behind, hold = tie(ahead, behind, beside[step - 2])
            swapped.append(lax.ppermute(hold, "pcol", SWAP))
        ahead, behind = up(ahead), down(behind)
        found = [(-step, ahead), (step, behind)]
        for offset, block in near:
            total = add(total, offset, block)
        if beside:
            ahead, behind, total = tie(ahead, behind, total)
        if 2 <= step < 2 + len(beside):
            ahead, behind, swapped[-1] = tie(ahead, behind, swapped[-1])
    last = move(jnp.where(core == 0, ahead, behind), SPLIT)
    for offset, block in found:
        total = add(total, offset, block)
    return add(total, NZ // 2, last), swapped


def z_two(piece, opposite, add, total, beside):
    one = up(piece), down(piece)
    three = up(opposite), down(opposite)
    total = add(total, 0, piece)
    *one, total = tie(*one, total)
    two = up(one[0]), down(one[1])
    swapped = []
    for block, after in zip(beside, one):
        block, _ = tie(block, after)
        swapped.append(lax.ppermute(block, "pcol", SWAP))
    total = add(total, NZ // 2, opposite)
    for offset, blocks in ((1, one), (-3, three), (2, two)):
        total = add(total, -offset, blocks[0])
        total = add(total, offset, blocks[1])
    return total, swapped


def on_device(anc_inverse, factor_panel, diag_inverse, block_pattern):
    p = lax.axis_index("prow")
    q = lax.axis_index("pcol")
    yh, x, c = p // 8, (p // 2) % NX, p % 2
    z, yl = q // 2, q % 2
    anc = anc_inverse.reshape(2, 256, 256)
    panel = factor_panel.reshape(2, 256, 256)
    diag = diag_inverse.reshape(2, 256, 256)

    def mine(pair):
        return jnp.where(yl == 0, pair[0], pair[1])

    def other(pair):
        return jnp.where(yl == 0, pair[1], pair[0])

    def swap(block):
        return lax.ppermute(block, "pcol", SWAP)

    near = move(
        jnp.where(c == 0, anc[0], anc[1]),
        both_perm(lambda chip, c, z, yl: (chip, yl, z, c)),
    )
    far = move(
        jnp.where(c == 0, anc[1], anc[0]),
        both_perm(lambda chip, c, z, yl: (chip, yl, z, 1 - c)),
    )
    oth_u, near = tie(other(panel), near)
    own_u, got_u = mine(panel), swap(oth_u)
    same = yl == c
    keep = lax.dynamic_slice(block_pattern, (yl, p - c, 2 * z + c), (1, 2, 1))
    keep = jnp.where(c == 0, keep, keep[:, ::-1]).reshape(2, 1, 1) != 0
    m_piece = jnp.where(same, jnp.stack([near, far]), jnp.stack([far, near]))
    m_piece = jnp.where(keep, m_piece, jnp.zeros_like(m_piece)).reshape(512, 256)

    u_piece = jnp.concatenate(
        [jnp.where(same, own_u, got_u), jnp.where(same, got_u, own_u)], axis=1
    )

    def along_x(block, step):
        return lax.ppermute(block, "prow", row_perm(lambda h, x, c: (h, x + step, c)))

    u_far = lax.ppermute(u_piece, "prow", FLIP_H)
    u_two = along_x(u_piece, 2)
    both = jnp.stack([u_piece, u_far])
    u_one = along_x(both, 1)
    u_three = along_x(both, 3)
    u_two_far = lax.ppermute(u_two, "prow", FLIP_H)
    u_all = jnp.zeros((NX, 2, 256, 512), jnp.bfloat16)
    for back, away, block in (
        (0, 0, both),
        (2, 0, u_two[None]),
        (2, 1, u_two_far[None]),
        (1, 0, u_one),
        (3, 0, u_three),
    ):
        u_all = lax.dynamic_update_slice(u_all, block[None], (back, away, 0, 0))

    def find(owner):
        owner = (owner + NZ) % NZ
        back = (x - owner % NX + NX) % NX
        return back, jnp.where(owner // NX == yh, 0, 1)

    def u_rows(panel, owner):
        at = (*find(owner), 0, 0)
        return lax.dynamic_slice(panel, at, (1, 1, 256, 512)).reshape(256, 512)

    def add_product(total, offset, block):
        rows = u_rows(u_all, z + offset)
        return tuple(
            part + jnp.dot(block, cols, preferred_element_type=jnp.float32)
            for part, cols in zip(total, (rows[:, :256], rows[:, 256:]))
        )

    zero = jnp.zeros((512, 256), jnp.float32)
    (kept, sent), _ = z_ring(m_piece, c, add_product, (zero, zero))
    theirs = lax.ppermute(sent, "prow", CROSS)
    off = kept + jnp.concatenate([theirs[256:], theirs[:256]], axis=0)
    off = (-off).astype(jnp.bfloat16)

    o_piece = move(off, both_perm(lambda chip, c, z, yl: (z, c, LAND[chip][z], yl)))
    o_other = move(off, both_perm(lambda chip, c, z, yl: (z, c, LAND[chip][z] + 4, yl)))
    u_cross = lax.ppermute(u_all, "prow", CROSS)
    o_piece, o_other, u_cross = tie(o_piece, o_other, u_cross)
    (u_cross,) = tie(jnp.where(p >= 0, u_cross, jnp.zeros_like(u_cross)))
    first, second = off[:256], lax.ppermute(off[256:], "prow", CROSS)
    off_mine = jnp.where(same, first, second)

    landed = sum(
        jnp.where(p // 2 == col, parts, 0) for col, parts in enumerate(LANDED)
    )

    def add_inner(total, offset, block):
        owner = (landed >> (3 * ((z + offset + NZ) % NZ))) & 7
        return tuple(
            part
            + lax.dot_general(
                u_rows(panel, owner),
                rows,
                (((0,), (0,)), ((), ())),
                preferred_element_type=jnp.float32,
            )
            for part, panel, rows in zip(
                total, (u_all, u_cross), (block[:256], block[256:])
            )
        )

    total, (off_got, d_got) = z_two(
        o_piece, o_other, add_inner, (zero, zero), (jnp.where(same, second, first), other(diag))
    )
    first = total[0][:256] + total[1][256:]
    second = total[0][256:] + total[1][:256]
    d_mine = mine(diag)
    diag_mine = (
        d_mine.astype(jnp.float32) - jnp.where(same, first, second)
    ).astype(jnp.bfloat16)
    diag_got = swap(
        (d_got.astype(jnp.float32) - jnp.where(same, second, first)).astype(
            jnp.bfloat16
        )
    )

    def place(own, got):
        return jnp.stack(
            [jnp.where(yl == 0, own, got), jnp.where(yl == 0, got, own)]
        ).reshape(anc_inverse.shape)

    return place(off_mine, off_got), place(diag_mine, diag_got)


def solution(mesh):
    return jax.shard_map(
        on_device,
        mesh=mesh,
        in_specs=(
            P(None, None, "prow", None, None, "pcol", None),
            P(None, None, "prow", None, None, "pcol", None),
            P(None, None, "pcol", None, None, "prow", None),
            P(),
        ),
        out_specs=(
            P(None, None, "prow", None, None, "pcol", None),
            P(None, None, "pcol", None, None, "prow", None),
        ),
        check_vma=False,
    )
```

```python
import jax
import jax.numpy as jnp
from jax import lax
from jax.sharding import PartitionSpec as P

NX = 4
NZ = 8


def row_perm(fn):
    pairs = []
    for i in range(16):
        yh, x, c = fn(i // 8, (i // 2) % NX, i % 2)
        pairs.append((i, yh * 8 + (x % NX) * 2 + c))
    return pairs


def col_perm(fn):
    pairs = []
    for i in range(16):
        z, yl = fn(i // 2, i % 2)
        pairs.append((i, (z % NZ) * 2 + yl))
    return pairs


def both_perm(fn):
    pairs = []
    for p in range(16):
        for q in range(16):
            chip, c, z, yl = fn(p // 2, p % 2, q // 2, q % 2)
            pairs.append((p * 16 + q, (chip * 2 + c) * 16 + (z % NZ) * 2 + yl))
    return pairs


LAND = (
    (1, 4, 7, 6, 1, 0, 3, 2),
    (7, 6, 1, 4, 2, 3, 0, 1),
    (6, 5, 0, 7, 3, 1, 2, 0),
    (4, 3, 6, 1, 4, 6, 1, 7),
    (3, 1, 2, 0, 7, 5, 6, 4),
    (0, 2, 3, 5, 6, 7, 5, 3),
    (5, 7, 4, 2, 5, 4, 7, 6),
    (2, 0, 5, 3, 0, 2, 4, 5),
)
LANDED = [
    sum(p << (3 * LAND[p][col]) for p in range(NZ)) for col in range(NZ)
]


def move(block, pairs):
    return lax.ppermute(block, ("prow", "pcol"), pairs)


SWAP = col_perm(lambda z, yl: (z, 1 - yl))
UP = col_perm(lambda z, yl: (z + 1, yl))
DOWN = col_perm(lambda z, yl: (z - 1, yl))
OPPOSITE = col_perm(lambda z, yl: (z + NZ // 2, yl))
CROSS = row_perm(lambda h, x, c: (h, x, 1 - c))
FLIP_H = row_perm(lambda h, x, c: (1 - h, x, c))
SPLIT = both_perm(lambda chip, c, z, yl: (chip, c, z + 1 - 2 * c, yl))


def up(block):
    return lax.ppermute(block, "pcol", UP)


def down(block):
    return lax.ppermute(block, "pcol", DOWN)


def tie(*values):
    return lax.optimization_barrier(values)


def z_ring(piece, core, add, total, beside=()):
    swapped = []
    ahead = behind = piece
    found = [(0, piece)]
    for step in range(1, NZ // 2):
        near = found
        if 2 <= step < 2 + len(beside):
            ahead, behind, hold = tie(ahead, behind, beside[step - 2])
            swapped.append(lax.ppermute(hold, "pcol", SWAP))
        ahead, behind = up(ahead), down(behind)
        found = [(-step, ahead), (step, behind)]
        for offset, block in near:
            total = add(total, offset, block)
        if beside:
            ahead, behind, total = tie(ahead, behind, total)
        if 2 <= step < 2 + len(beside):
            ahead, behind, swapped[-1] = tie(ahead, behind, swapped[-1])
    last = move(jnp.where(core == 0, ahead, behind), SPLIT)
    for offset, block in found:
        total = add(total, offset, block)
    return add(total, NZ // 2, last), swapped


def z_two(piece, opposite, add, total, beside):
    one = up(piece), down(piece)
    three = up(opposite), down(opposite)
    total = add(total, 0, piece)
    *one, total = tie(*one, total)
    two = up(one[0]), down(one[1])
    swapped = []
    for block, after in zip(beside, one):
        block, _ = tie(block, after)
        swapped.append(lax.ppermute(block, "pcol", SWAP))
    total = add(total, NZ // 2, opposite)
    for offset, blocks in ((1, one), (-3, three), (2, two)):
        total = add(total, -offset, blocks[0])
        total = add(total, offset, blocks[1])
    return total, swapped


def on_device(anc_inverse, factor_panel, diag_inverse, block_pattern):
    p = lax.axis_index("prow")
    q = lax.axis_index("pcol")
    yh, x, c = p // 8, (p // 2) % NX, p % 2
    z, yl = q // 2, q % 2
    anc = anc_inverse.reshape(2, 256, 256)
    panel = factor_panel.reshape(2, 256, 256)
    diag = diag_inverse.reshape(2, 256, 256)

    def mine(pair):
        return jnp.where(yl == 0, pair[0], pair[1])

    def other(pair):
        return jnp.where(yl == 0, pair[1], pair[0])

    def swap(block):
        return lax.ppermute(block, "pcol", SWAP)

    near = move(
        jnp.where(c == 0, anc[0], anc[1]),
        both_perm(lambda chip, c, z, yl: (chip, yl, z, c)),
    )
    far = move(
        jnp.where(c == 0, anc[1], anc[0]),
        both_perm(lambda chip, c, z, yl: (chip, yl, z, 1 - c)),
    )
    oth_u, near = tie(other(panel), near)
    own_u, got_u = mine(panel), swap(oth_u)
    same = yl == c
    keep = lax.dynamic_slice(block_pattern, (yl, p - c, 2 * z + c), (1, 2, 1))
    keep = jnp.where(c == 0, keep, keep[:, ::-1]).reshape(2, 1, 1) != 0
    m_piece = jnp.where(same, jnp.stack([near, far]), jnp.stack([far, near]))
    m_piece = jnp.where(keep, m_piece, jnp.zeros_like(m_piece)).reshape(512, 256)

    u_piece = jnp.concatenate(
        [jnp.where(same, own_u, got_u), jnp.where(same, got_u, own_u)], axis=1
    )

    def along_x(block, step):
        return lax.ppermute(block, "prow", row_perm(lambda h, x, c: (h, x + step, c)))

    u_far = lax.ppermute(u_piece, "prow", FLIP_H)
    u_two = along_x(u_piece, 2)
    both = jnp.stack([u_piece, u_far])
    u_one = along_x(both, 1)
    u_three = along_x(both, 3)
    u_two_far = lax.ppermute(u_two, "prow", FLIP_H)
    u_all = jnp.zeros((NX, 2, 256, 512), jnp.bfloat16)
    for back, away, block in (
        (0, 0, both),
        (2, 0, u_two[None]),
        (2, 1, u_two_far[None]),
        (1, 0, u_one),
        (3, 0, u_three),
    ):
        u_all = lax.dynamic_update_slice(u_all, block[None], (back, away, 0, 0))

    def find(owner):
        owner = (owner + NZ) % NZ
        back = (x - owner % NX + NX) % NX
        return back, jnp.where(owner // NX == yh, 0, 1)

    def u_rows(panel, owner):
        at = (*find(owner), 0, 0)
        return lax.dynamic_slice(panel, at, (1, 1, 256, 512)).reshape(256, 512)

    def add_product(total, offset, block):
        rows = u_rows(u_all, z + offset)
        return tuple(
            part + jnp.dot(block, cols, preferred_element_type=jnp.float32)
            for part, cols in zip(total, (rows[:, :256], rows[:, 256:]))
        )

    zero = jnp.zeros((512, 256), jnp.float32)
    (kept, sent), _ = z_ring(m_piece, c, add_product, (zero, zero))
    theirs = lax.ppermute(sent, "prow", CROSS)
    off = kept + jnp.concatenate([theirs[256:], theirs[:256]], axis=0)
    off = (-off).astype(jnp.bfloat16)

    o_piece = move(off, both_perm(lambda chip, c, z, yl: (z, c, LAND[chip][z], yl)))
    o_other = move(off, both_perm(lambda chip, c, z, yl: (z, c, LAND[chip][z] + 4, yl)))
    u_cross = lax.ppermute(u_all, "prow", CROSS)
    o_piece, o_other, u_cross = tie(o_piece, o_other, u_cross)
    (u_cross,) = tie(jnp.where(p >= 0, u_cross, jnp.zeros_like(u_cross)))
    first, second = off[:256], lax.ppermute(off[256:], "prow", CROSS)
    off_mine = jnp.where(same, first, second)

    landed = sum(
        jnp.where(p // 2 == col, parts, 0) for col, parts in enumerate(LANDED)
    )

    def add_inner(total, offset, block):
        owner = (landed >> (3 * ((z + offset + NZ) % NZ))) & 7
        return tuple(
            part
            + lax.dot_general(
                u_rows(panel, owner),
                rows,
                (((0,), (0,)), ((), ())),
                preferred_element_type=jnp.float32,
            )
            for part, panel, rows in zip(
                total, (u_all, u_cross), (block[:256], block[256:])
            )
        )

    beside = jnp.stack([jnp.where(same, second, first), other(diag)])
    total, (got,) = z_two(o_piece, o_other, add_inner, (zero, zero), (beside,))
    off_got, d_got = got[0], got[1]
    first = total[0][:256] + total[1][256:]
    second = total[0][256:] + total[1][:256]
    d_mine = mine(diag)
    diag_mine = (
        d_mine.astype(jnp.float32) - jnp.where(same, first, second)
    ).astype(jnp.bfloat16)
    diag_got = swap(
        (d_got.astype(jnp.float32) - jnp.where(same, second, first)).astype(
            jnp.bfloat16
        )
    )

    def place(own, got):
        return jnp.stack(
            [jnp.where(yl == 0, own, got), jnp.where(yl == 0, got, own)]
        ).reshape(anc_inverse.shape)

    return place(off_mine, off_got), place(diag_mine, diag_got)


def solution(mesh):
    return jax.shard_map(
        on_device,
        mesh=mesh,
        in_specs=(
            P(None, None, "prow", None, None, "pcol", None),
            P(None, None, "prow", None, None, "pcol", None),
            P(None, None, "pcol", None, None, "prow", None),
            P(),
        ),
        out_specs=(
            P(None, None, "prow", None, None, "pcol", None),
            P(None, None, "pcol", None, None, "prow", None),
        ),
        check_vma=False,
    )
```

```python
import jax
import jax.numpy as jnp
from jax import lax
from jax.sharding import PartitionSpec as P

NX = 4
NZ = 8


def row_perm(fn):
    pairs = []
    for i in range(16):
        yh, x, c = fn(i // 8, (i // 2) % NX, i % 2)
        pairs.append((i, yh * 8 + (x % NX) * 2 + c))
    return pairs


def col_perm(fn):
    pairs = []
    for i in range(16):
        z, yl = fn(i // 2, i % 2)
        pairs.append((i, (z % NZ) * 2 + yl))
    return pairs


def both_perm(fn):
    pairs = []
    for p in range(16):
        for q in range(16):
            chip, c, z, yl = fn(p // 2, p % 2, q // 2, q % 2)
            pairs.append((p * 16 + q, (chip * 2 + c) * 16 + (z % NZ) * 2 + yl))
    return pairs


LAND = (
    (1, 4, 7, 6, 1, 0, 3, 2),
    (7, 6, 1, 4, 2, 3, 0, 1),
    (6, 5, 0, 7, 3, 1, 2, 0),
    (4, 3, 6, 1, 4, 6, 1, 7),
    (3, 1, 2, 0, 7, 5, 6, 4),
    (0, 2, 3, 5, 6, 7, 5, 3),
    (5, 7, 4, 2, 5, 4, 7, 6),
    (2, 0, 5, 3, 0, 2, 4, 5),
)
LANDED = [
    sum(p << (3 * LAND[p][col]) for p in range(NZ)) for col in range(NZ)
]


def move(block, pairs):
    return lax.ppermute(block, ("prow", "pcol"), pairs)


SWAP = col_perm(lambda z, yl: (z, 1 - yl))
UP = col_perm(lambda z, yl: (z + 1, yl))
DOWN = col_perm(lambda z, yl: (z - 1, yl))
OPPOSITE = col_perm(lambda z, yl: (z + NZ // 2, yl))
CROSS = row_perm(lambda h, x, c: (h, x, 1 - c))
FLIP_H = row_perm(lambda h, x, c: (1 - h, x, c))
SPLIT = both_perm(lambda chip, c, z, yl: (chip, c, z + 1 - 2 * c, yl))


def up(block):
    return lax.ppermute(block, "pcol", UP)


def down(block):
    return lax.ppermute(block, "pcol", DOWN)


def tie(*values):
    return lax.optimization_barrier(values)


def z_ring(piece, core, add, total, beside=()):
    swapped = []
    ahead = behind = piece
    found = [(0, piece)]
    for step in range(1, NZ // 2):
        near = found
        if 2 <= step < 2 + len(beside):
            ahead, behind, hold = tie(ahead, behind, beside[step - 2])
            swapped.append(lax.ppermute(hold, "pcol", SWAP))
        ahead, behind = up(ahead), down(behind)
        found = [(-step, ahead), (step, behind)]
        for offset, block in near:
            total = add(total, offset, block)
        if beside:
            ahead, behind, total = tie(ahead, behind, total)
        if 2 <= step < 2 + len(beside):
            ahead, behind, swapped[-1] = tie(ahead, behind, swapped[-1])
    last = move(jnp.where(core == 0, ahead, behind), SPLIT)
    for offset, block in found:
        total = add(total, offset, block)
    return add(total, NZ // 2, last), swapped


def z_two(piece, opposite, add, total, beside):
    one = up(piece), down(piece)
    three = up(opposite), down(opposite)
    total = add(total, 0, piece)
    *one, total = tie(*one, total)
    two = up(one[0]), down(one[1])
    swapped = []
    for block, after in zip(beside, (one[0], three[0])):
        block, _ = tie(block, after)
        swapped.append(lax.ppermute(block, "pcol", SWAP))
    total = add(total, NZ // 2, opposite)
    for offset, blocks in ((1, one), (-3, three), (2, two)):
        total = add(total, -offset, blocks[0])
        total = add(total, offset, blocks[1])
    return total, swapped


def on_device(anc_inverse, factor_panel, diag_inverse, block_pattern):
    p = lax.axis_index("prow")
    q = lax.axis_index("pcol")
    yh, x, c = p // 8, (p // 2) % NX, p % 2
    z, yl = q // 2, q % 2
    anc = anc_inverse.reshape(2, 256, 256)
    panel = factor_panel.reshape(2, 256, 256)
    diag = diag_inverse.reshape(2, 256, 256)

    def mine(pair):
        return jnp.where(yl == 0, pair[0], pair[1])

    def other(pair):
        return jnp.where(yl == 0, pair[1], pair[0])

    def swap(block):
        return lax.ppermute(block, "pcol", SWAP)

    near = move(
        jnp.where(c == 0, anc[0], anc[1]),
        both_perm(lambda chip, c, z, yl: (chip, yl, z, c)),
    )
    far = move(
        jnp.where(c == 0, anc[1], anc[0]),
        both_perm(lambda chip, c, z, yl: (chip, yl, z, 1 - c)),
    )
    oth_u, near = tie(other(panel), near)
    own_u, got_u = mine(panel), swap(oth_u)
    same = yl == c
    keep = lax.dynamic_slice(block_pattern, (yl, p - c, 2 * z + c), (1, 2, 1))
    keep = jnp.where(c == 0, keep, keep[:, ::-1]).reshape(2, 1, 1) != 0
    m_piece = jnp.where(same, jnp.stack([near, far]), jnp.stack([far, near]))
    m_piece = jnp.where(keep, m_piece, jnp.zeros_like(m_piece)).reshape(512, 256)

    u_piece = jnp.concatenate(
        [jnp.where(same, own_u, got_u), jnp.where(same, got_u, own_u)], axis=1
    )

    def along_x(block, step):
        return lax.ppermute(block, "prow", row_perm(lambda h, x, c: (h, x + step, c)))

    u_far = lax.ppermute(u_piece, "prow", FLIP_H)
    u_two = along_x(u_piece, 2)
    both = jnp.stack([u_piece, u_far])
    u_one = along_x(both, 1)
    u_three = along_x(both, 3)
    u_two_far = lax.ppermute(u_two, "prow", FLIP_H)
    u_all = jnp.zeros((NX, 2, 256, 512), jnp.bfloat16)
    for back, away, block in (
        (0, 0, both),
        (2, 0, u_two[None]),
        (2, 1, u_two_far[None]),
        (1, 0, u_one),
        (3, 0, u_three),
    ):
        u_all = lax.dynamic_update_slice(u_all, block[None], (back, away, 0, 0))

    def find(owner):
        owner = (owner + NZ) % NZ
        back = (x - owner % NX + NX) % NX
        return back, jnp.where(owner // NX == yh, 0, 1)

    def u_rows(panel, owner):
        at = (*find(owner), 0, 0)
        return lax.dynamic_slice(panel, at, (1, 1, 256, 512)).reshape(256, 512)

    def add_product(total, offset, block):
        rows = u_rows(u_all, z + offset)
        return tuple(
            part + jnp.dot(block, cols, preferred_element_type=jnp.float32)
            for part, cols in zip(total, (rows[:, :256], rows[:, 256:]))
        )

    zero = jnp.zeros((512, 256), jnp.float32)
    (kept, sent), _ = z_ring(m_piece, c, add_product, (zero, zero))
    theirs = lax.ppermute(sent, "prow", CROSS)
    off = kept + jnp.concatenate([theirs[256:], theirs[:256]], axis=0)
    off = (-off).astype(jnp.bfloat16)

    o_piece = move(off, both_perm(lambda chip, c, z, yl: (z, c, LAND[chip][z], yl)))
    o_other = move(off, both_perm(lambda chip, c, z, yl: (z, c, LAND[chip][z] + 4, yl)))
    u_cross = lax.ppermute(u_all, "prow", CROSS)
    o_piece, o_other, u_cross = tie(o_piece, o_other, u_cross)
    (u_cross,) = tie(jnp.where(p >= 0, u_cross, jnp.zeros_like(u_cross)))
    first, second = off[:256], lax.ppermute(off[256:], "prow", CROSS)
    off_mine = jnp.where(same, first, second)

    landed = sum(
        jnp.where(p // 2 == col, parts, 0) for col, parts in enumerate(LANDED)
    )

    def add_inner(total, offset, block):
        owner = (landed >> (3 * ((z + offset + NZ) % NZ))) & 7
        return tuple(
            part
            + lax.dot_general(
                u_rows(panel, owner),
                rows,
                (((0,), (0,)), ((), ())),
                preferred_element_type=jnp.float32,
            )
            for part, panel, rows in zip(
                total, (u_all, u_cross), (block[:256], block[256:])
            )
        )

    total, (off_got, d_got) = z_two(
        o_piece, o_other, add_inner, (zero, zero), (jnp.where(same, second, first), other(diag))
    )
    first = total[0][:256] + total[1][256:]
    second = total[0][256:] + total[1][:256]
    d_mine = mine(diag)
    diag_mine = (
        d_mine.astype(jnp.float32) - jnp.where(same, first, second)
    ).astype(jnp.bfloat16)
    diag_got = swap(
        (d_got.astype(jnp.float32) - jnp.where(same, second, first)).astype(
            jnp.bfloat16
        )
    )

    def place(own, got):
        return jnp.stack(
            [jnp.where(yl == 0, own, got), jnp.where(yl == 0, got, own)]
        ).reshape(anc_inverse.shape)

    return place(off_mine, off_got), place(diag_mine, diag_got)


def solution(mesh):
    return jax.shard_map(
        on_device,
        mesh=mesh,
        in_specs=(
            P(None, None, "prow", None, None, "pcol", None),
            P(None, None, "prow", None, None, "pcol", None),
            P(None, None, "pcol", None, None, "prow", None),
            P(),
        ),
        out_specs=(
            P(None, None, "prow", None, None, "pcol", None),
            P(None, None, "pcol", None, None, "prow", None),
        ),
        check_vma=False,
    )
```
